32 devices in a mesh: field: 2 (over y), ccd: 16 (over z, x, core).
Axes of the slice: x: 2, y: 2, z: 4, core: 2. Of those that a mesh axis runs over, the one named last changes fastest.
Arguments:
- exposures: float32 [2, 4096, 1024], P(None, ('field', 'ccd')), parts along dimension 1, may hold values from -100 to 100
- lanczos_shift: int32 [2, 32, 2], P(None, ('field', 'ccd')), parts along dimension 1, may hold values from -2 to 2
- lanczos_frac: float32 [2, 32, 2], P(None, ('field', 'ccd')), parts along dimension 1, may hold values from 0 to 1
- margin_patch: int32 [32, 32, 1], P('field'), parts along dimension 0, may hold values from 0 to 15; in each aligned block of 32 rows (0 to 31, 32 to 63, ..., all dimensions but the last counted through in order) at most 4 rows name the same one
- margin_slot: int32 [32, 32], P('field'), parts along dimension 0, may hold values from 0 to 31
Outputs:
- difference: float32 [4096, 1024], P(('field', 'ccd')), parts along dimension 0
The draws below stay inside these ranges and needn't reach their ends.
There are 2 independent parts, one for each index of `field`. The reference program is written for one: setup_inputs(seed, part) draws one part's arguments, and reference() takes and returns one part's arrays. A program takes and returns all parts, laid end to end along the dimension named above; each array names one. Nothing has to cross between parts.
Inputs may be any that keep to these rules, and one draw needn't show every extreme that they name: `margin_patch`: no CCD has more than 4 of its blocks on one patch, and some CCD has exactly 4 on one patch; every patch is intersected by some block.
All inputs are finite; a program needn't handle non-finite values.
Results may differ from the reference program's by a relative error of at most 0.0003.
Values sent between devices are 32-bit elements; how exact they have to be, the bound alone decides.
A program may use at most 128 MiB of HBM per device.

```python
import math
import jax
import jax.numpy as jnp
import numpy as np
from jax import lax

TR = 128
TC = 1024
BR = 32
BC = 128
KSIDE = 5
KB = 25
NB = 32
NCCD = 16
CAP = 4


def draw_exposures(key, part):
    key_sky, key_gain, key_noise = jax.random.split(jax.random.fold_in(key, 71), 3)
    sky = jnp.clip(jax.random.normal(key_sky, (NCCD, TR, TC), jnp.float32), -6.0, 6.0)
    sides = jnp.roll(sky, 1, 1) + jnp.roll(sky, -1, 1) + jnp.roll(sky, 1, 2) + jnp.roll(sky, -1, 2)
    corners = jnp.roll(jnp.roll(sky, 1, 1), 1, 2) + jnp.roll(jnp.roll(sky, 1, 1), -1, 2)
    corners = corners + jnp.roll(jnp.roll(sky, -1, 1), 1, 2) + jnp.roll(jnp.roll(sky, -1, 1), -1, 2)
    blurred = 0.25 * sky + 0.125 * sides + 0.0625 * corners
    ramp = 1.0 + 2.0 * jnp.arange(NCCD).astype(jnp.float32) / max(NCCD - 1, 1)
    gains = ramp[:, None, None] * jax.random.uniform(key_gain, (NCCD, 1, 1), jnp.float32, 0.8, 1.2)
    noise = 0.5 * jnp.clip(jax.random.normal(key_noise, (NCCD, TR, TC), jnp.float32), -6.0, 6.0)
    science = gains * blurred + noise
    return jnp.stack([sky, science]).reshape(2, NCCD * TR, TC).astype(jnp.float32)


def place_ends(entries, key, least, largest):
    place = [jax.random.randint(jax.random.fold_in(key, axis), (), 0, length) for axis, length in enumerate(entries.shape)]
    widest = entries.shape.index(max(entries.shape))
    beside = place[:widest] + [(place[widest] + 1) % entries.shape[widest]] + place[widest + 1:]
    return entries.at[tuple(place)].set(least).at[tuple(beside)].set(largest)


def level_of(rng, dims, cuts, low, top_value):
    gain, own = 1.0, jax.random.fold_in(rng, 6)
    for dim, parts in cuts:
        heights = jnp.exp(jax.random.uniform(jax.random.fold_in(own, dim), (parts,), jnp.float32, low / len(cuts), top_value / len(cuts)))
        gain = gain * jnp.repeat(heights, dims[dim] // parts).reshape([-1 if axis == dim else 1 for axis in range(len(dims))])
    return gain


def routed_block(stream_key, own, number, rows, amount, top, most, skew):
    order = jax.random.permutation(stream_key, amount)
    heavy_load, common = portions_of(amount, rows * top, most, skew, True), portions_of(amount, rows * top, most, skew, False)
    places = jnp.arange(amount)

    def named(lengths, turn):
        used = int((lengths > 0).sum())
        fixed = max(1, used // 4)
        passed = fixed + (places - fixed + turn * (used - fixed)) % max(1, amount - fixed)
        return jnp.zeros((amount,), jnp.int32).at[order[jnp.where(places < fixed, places, passed)]].set(jnp.asarray(lengths, jnp.int32))

    lengths = jnp.where(number % 4 == 0, named(heavy_load, number // 4), named(common, number - number // 4 - 1))
    mixed = jax.random.permutation(jax.random.fold_in(own, 3), amount)
    donor, receiver = mixed[0:amount // 2 * 2:2], mixed[1:amount // 2 * 2:2]
    room = jnp.minimum(lengths[donor] - 1, most - lengths[receiver]) // 2
    room = jnp.where((donor == order[0]) | (receiver == order[0]) | (lengths[receiver] == 0), 0, jnp.maximum(room, 0))
    passed = jax.random.randint(jax.random.fold_in(own, 4), (amount // 2,), 0, 1 << 20) % (room + 1)
    lengths = lengths.at[donor].add(-passed).at[receiver].add(passed)
    members = jnp.searchsorted(jnp.cumsum(lengths), jnp.arange(rows * top), side="right").astype(jnp.int32)
    table = members.reshape(top, rows).T
    table = table[jax.random.permutation(jax.random.fold_in(own, 1), rows)]
    turn = jax.random.randint(jax.random.fold_in(own, 2), (rows, 1), 0, top)
    return jnp.take_along_axis(table, (jnp.arange(top)[None, :] + turn) % top, axis=1)


def portions_of(number_of, total, most, lean, full):
    weights = [(1 << 20) // math.isqrt(standing ** lean) + 1 for standing in range(1, number_of + 1)]
    largest = most if full else min(most, max(-(-total // number_of), total * weights[0] // sum(weights)))
    least = 1 if total - largest >= number_of - 1 else 0
    given, spare = [largest] + [least] * (number_of - 1), total - largest - least * (number_of - 1)
    while spare > 0:
        movable = [i for i in range(1, number_of) if given[i] < largest] or [i for i in range(1, number_of) if given[i] < most]
        whole, remaining = sum([weights[i] for i in movable]), spare
        for i in movable:
            extra = min(most - given[i], max(1, remaining * weights[i] // whole), spare)
            given[i] = given[i] + extra
            spare = spare - extra
    return np.array(given)


def setup_inputs(seed: int = 0, part: int = 0) -> dict:
    key_list = jax.random.split(jax.random.key(seed), 6)
    part_keys = jax.random.split(jax.random.fold_in(key_list[5], part), 6)
    exposures = draw_exposures(jax.random.fold_in(jax.random.fold_in(key_list[5], part), 71), part)
    lanczos_shift = place_ends(jax.random.randint(part_keys[1], (2, NCCD, 2), -2, 3), jax.random.fold_in(part_keys[1], 1), -2, 2).astype(jnp.int32)
    lanczos_frac = jnp.clip(1.0 * jax.random.uniform(part_keys[2], (2, NCCD, 2), jnp.float32) ** level_of(part_keys[2], (2, NCCD, 2), ((1, 16),), -0.2, 0.2), 0.0, 1.0)
    margin_patch_keys = jax.random.split(jax.random.fold_in(part_keys[3], 1), NCCD * NB // NB)
    margin_patch_turns = jax.random.permutation(jax.random.fold_in(part_keys[3], 3), NCCD * NB // NB)
    margin_patch = jax.vmap(lambda own, number: routed_block(jax.random.fold_in(part_keys[3], 2), own, number, NB, NCCD, 1, CAP, 2))(margin_patch_keys, margin_patch_turns).reshape((NCCD, NB, 1))
    margin_slot = place_ends(jax.random.randint(part_keys[4], (NCCD, NB), 0, NB), jax.random.fold_in(part_keys[4], 1), 0, NB - 1).astype(jnp.int32)
    return dict(exposures=exposures, lanczos_shift=lanczos_shift, lanczos_frac=lanczos_frac, margin_patch=margin_patch, margin_slot=margin_slot)


def lanczos_matrix(length, shift, frac):
    positions = jnp.arange(length).astype(jnp.float32)
    offset = positions[None, :] - positions[:, None] - shift.astype(jnp.float32) - frac
    taper = jnp.sinc(offset) * jnp.sinc(offset / 3.0)
    return jnp.where(jnp.abs(offset) < 3.0, taper, jnp.zeros_like(taper))

def resample_tile(tile, shift, frac):
    row_weights = lanczos_matrix(tile.shape[0], shift[0], frac[0])
    col_weights = lanczos_matrix(tile.shape[1], shift[1], frac[1])
    inner = jnp.dot(row_weights, tile, precision=lax.Precision.HIGHEST)
    return jnp.dot(inner, col_weights.T, precision=lax.Precision.HIGHEST)

def coadd_visit(raw, shifts, fracs, segment_ids):
    tiles = raw.reshape(NCCD, TR, TC)

    def warp_one(items):
        return resample_tile(items[0], items[1], items[2])
    warped = lax.map(warp_one, (tiles, shifts, fracs))
    pieces = warped.reshape(NCCD, TR // BR, BR, TC // BC, BC).transpose(0, 1, 3, 2, 4).reshape(NCCD * NB, BR * BC)
    summed = jax.ops.segment_sum(pieces, segment_ids, num_segments=NCCD * NB)
    return summed.reshape(NCCD, TR // BR, TC // BC, BR, BC).transpose(0, 1, 3, 2, 4).reshape(NCCD * TR, TC)

def reference(exposures, lanczos_shift, lanczos_frac, margin_patch, margin_slot):
    segment_ids = (margin_patch[:, :, 0] * NB + margin_slot).reshape(-1).astype(jnp.int32)
    template = coadd_visit(exposures[0], lanczos_shift[0], lanczos_frac[0], segment_ids)
    science = coadd_visit(exposures[1], lanczos_shift[1], lanczos_frac[1], segment_ids)
    reach = KSIDE // 2
    padded_image = jnp.pad(template, reach)
    total_rows = template.shape[0]
    columns = template.shape[1]

    def accumulate(index, carry):
        gram, rhs = carry
        first = (index * BR).astype(jnp.int32)
        window = lax.dynamic_slice(padded_image, (first, jnp.int32(0)), (BR + 2 * reach, columns + 2 * reach))
        stack = jnp.stack([window[r:r + BR, q:q + columns] for r in range(KSIDE) for q in range(KSIDE)]).reshape(KSIDE * KSIDE, BR * columns)
        target = lax.dynamic_slice_in_dim(science, first, BR, 0).reshape(-1)
        gram = gram + jnp.dot(stack, stack.T, precision=lax.Precision.HIGHEST)
        rhs = rhs + jnp.dot(stack, target, precision=lax.Precision.HIGHEST)
        return (gram, rhs)
    start = (jnp.zeros((KB, KB), jnp.float32), jnp.zeros((KB,), jnp.float32))
    gram, rhs = lax.fori_loop(0, total_rows // BR, accumulate, start)
    ridge = 0.001 * jnp.trace(gram) / KB + 1.0
    kernel = jnp.linalg.solve(gram + ridge * jnp.eye(KB, dtype=jnp.float32), rhs)
    model = jnp.zeros_like(science)
    for r in range(KSIDE):
        for q in range(KSIDE):
            model = model + kernel[r * KSIDE + q] * padded_image[r:r + total_rows, q:q + columns]
    return science - model
```

```python
import functools

import jax
import jax.numpy as jnp
from jax import lax
from jax.experimental import pallas as pl
from jax.experimental.pallas import tpu as pltpu
from jax.sharding import PartitionSpec as P

BR = 32
BC = 128
KSIDE = 5
KB = 25
NB = 32
REACH = KSIDE // 2
LOW, HIGH = -4, 5
TAPS = HIGH - LOW + 1
MESH = pl.DeviceIdType.MESH
VMEM_LIMIT = 56 * 1024 * 1024


def greet_all(n, me):
    barrier = pltpu.get_barrier_semaphore()

    @pl.loop(1, n)
    def _(i):
        pl.semaphore_signal(
            barrier, inc=1, device_id={"ccd": lax.rem(me + i, n)}, device_id_type=MESH
        )

    return barrier


def exchange_kernel(n, cap, taps_ref, index_ref, raw_ref, got_ref, rows_pad, warped, send,
                    send_sem, recv_sem, own_sem):
    me = lax.axis_index("ccd")
    barrier = greet_all(n, me)
    rows, columns = raw_ref.shape[1:]
    lanes = columns // BC
    bands = rows // BR
    rows_pad[:, 0:8, :] = jnp.zeros((lanes, 8, BC), jnp.float32)
    rows_pad[:, rows + 8 : rows + 16, :] = jnp.zeros((lanes, 8, BC), jnp.float32)

    def copy_to(v, i):
        partner = lax.rem(me + i, n)
        return pltpu.make_async_remote_copy(
            src_ref=send.at[v, partner],
            dst_ref=got_ref.at[v, me],
            send_sem=send_sem.at[v, partner],
            recv_sem=recv_sem.at[v, me],
            device_id={"ccd": partner},
            device_id_type=MESH,
        )

    def own_copy(v):
        return pltpu.make_async_copy(send.at[v, me], got_ref.at[v, me], own_sem.at[v])

    for v in range(2):

        @pl.loop(0, rows // 8)
        def _(c):
            start = pl.multiple_of(c * 8, 8)
            line = jnp.concatenate(
                [raw_ref[v, pl.ds(start, 8), :], jnp.zeros((8, BC), jnp.float32)], axis=1
            )
            width = columns + BC
            total = None
            for k in range(LOW, HIGH + 1):
                moved = line if k == 0 else pltpu.roll(line, (-k) % width, 1)
                term = taps_ref[v, 1, k - LOW] * moved[:, :columns]
                total = term if total is None else total + term
            for lb in range(lanes):
                rows_pad[lb, pl.ds(start + 8, 8), :] = total[:, lb * BC : (lb + 1) * BC]

        @pl.loop(0, lanes)
        def _(lb):
            for rb in range(bands):
                total = None
                for k in range(LOW, HIGH + 1):
                    first = 8 + rb * BR + k
                    term = taps_ref[v, 0, k - LOW] * rows_pad[lb, first : first + BR, :]
                    total = term if total is None else total + term
                warped[v, lb * bands + rb] = total

        @pl.loop(0, n)
        def _(p):
            for z in range(cap):
                send[v, p, z] = warped[v, index_ref[p * cap + z]]

        if v == 0:
            pl.semaphore_wait(barrier, n - 1)

        @pl.loop(1, n)
        def _(i):
            copy_to(v, i).start()

        own_copy(v).start()

    for v in range(2):
        own_copy(v).wait()

        @pl.loop(1, n)
        def _(i):
            copy_to(v, i).wait_send()
            source = lax.rem(me + n - i, n)
            pltpu.make_async_remote_copy(
                src_ref=send.at[v, source],
                dst_ref=got_ref.at[v, source],
                send_sem=send_sem.at[v, source],
                recv_sem=recv_sem.at[v, source],
                device_id={"ccd": source},
                device_id_type=MESH,
            ).wait_recv()


def coadd_kernel(count, place_ref, got_ref, template_ref, science_ref):
    for v, ref in ((0, template_ref), (1, science_ref)):
        ref[...] = jnp.zeros_like(ref)

        @pl.loop(0, count)
        def _(t):
            e = place_ref[t]
            ref[e] = ref[e] + got_ref[v, t]


def fit_kernel(n, t_ref, s_ref, out_ref, top, low, basis, entries, mine, gathered, weights,
               halo_send, halo_recv, fit_send, fit_recv):
    me = lax.axis_index("ccd")
    barrier = greet_all(n, me)
    lanes, rows = t_ref.shape[0], t_ref.shape[1]
    columns = lanes * BC
    groups = rows // 8
    right, left = lax.rem(me + 1, n), lax.rem(me + n - 1, n)
    entries[...] = jnp.zeros_like(entries)

    pl.semaphore_wait(barrier, n - 1)
    down = pltpu.make_async_remote_copy(
        src_ref=t_ref.at[:, pl.ds(rows - 8, 8), :], dst_ref=top,
        send_sem=halo_send.at[0], recv_sem=halo_recv.at[0],
        device_id={"ccd": right}, device_id_type=MESH,
    )
    up = pltpu.make_async_remote_copy(
        src_ref=t_ref.at[:, pl.ds(0, 8), :], dst_ref=low,
        send_sem=halo_send.at[1], recv_sem=halo_recv.at[1],
        device_id={"ccd": left}, device_id_type=MESH,
    )
    down.start()
    up.start()

    def shifted(pieces):
        line = jnp.concatenate(pieces + [jnp.zeros((8, BC), jnp.float32)], axis=1)
        for q in range(KSIDE):
            k = q - REACH
            yield q, line if k == 0 else pltpu.roll(line, (-k) % (columns + BC), 1)

    @pl.loop(0, groups)
    def _(g):
        start = pl.multiple_of(g * 8, 8)
        for q, line in shifted([t_ref[lb, pl.ds(start, 8), :] for lb in range(lanes)]):
            for lb in range(lanes):
                basis[q, lb, pl.ds(start + REACH, 8), :] = line[:, lb * BC : (lb + 1) * BC]

    down.wait()
    up.wait()
    has_top = (me > 0).astype(jnp.float32)
    has_low = (me < n - 1).astype(jnp.float32)
    for q, line in shifted([top[lb] * has_top for lb in range(lanes)]):
        for lb in range(lanes):
            basis[q, lb, 0:REACH, :] = line[8 - REACH : 8, lb * BC : (lb + 1) * BC]
    first = rows + REACH
    for q, line in shifted([low[lb] * has_low for lb in range(lanes)]):
        for lb in range(lanes):
            basis[q, lb, first : first + REACH, :] = line[0:REACH, lb * BC : (lb + 1) * BC]
            basis[q, lb, first + REACH : rows + 16, :] = jnp.zeros(
                (16 - 2 * REACH, BC), jnp.float32
            )

    sub = lax.broadcasted_iota(jnp.int32, (8, BC), 0)
    zero = jnp.zeros((8, BC), jnp.float32)

    for dr in range(KSIDE):

        @pl.loop(0, KSIDE)
        def _(qq):
            def add(start, sums, with_science=True):
                sums = list(sums)
                for lb in range(lanes):
                    other = basis[qq, lb, pl.ds(start + dr, 8), :]
                    for q in range(KSIDE):
                        sums[q] = sums[q] + basis[q, lb, pl.ds(start, 8), :] * other
                    if with_science:
                        sums[KSIDE] = sums[KSIDE] + s_ref[lb, pl.ds(start, 8), :] * other
                return tuple(sums)

            head = add(0, (zero,) * (KSIDE + 1))
            core = lax.fori_loop(
                1,
                groups,
                lambda g, sums: add(pl.multiple_of(g * 8, 8), sums),
                (zero,) * KSIDE + (head[KSIDE],),
            )
            tail = add(rows, (zero,) * KSIDE, False)
            entries[KB, pl.ds(dr * KSIDE + qq, 1), :] = jnp.sum(core[KSIDE], 0, keepdims=True)
            for r in range(KSIDE - dr):
                for q in range(KSIDE):
                    window = (
                        core[q]
                        + jnp.where(sub >= r, head[q], 0.0)
                        + jnp.where(sub < r, tail[q], 0.0)
                    )
                    line = jnp.sum(window, 0, keepdims=True)
                    here = (r + dr) * KSIDE + qq
                    entries[here, r * KSIDE + q : r * KSIDE + q + 1, :] = line
                    if dr > 0:
                        entries[r * KSIDE + q, pl.ds(here, 1), :] = line

    row_id = lax.broadcasted_iota(jnp.int32, (32, BC), 0)
    lane_id = lax.broadcasted_iota(jnp.int32, (32, BC), 1)
    part = jnp.zeros((32, BC), jnp.float32)
    for j in range(KB + 1):
        part = jnp.where(lane_id == j, jnp.sum(entries[j], 1, keepdims=True), part)
    mine[...] = part
    gathered[me] = part

    def share(i):
        partner = lax.rem(me + i, n)
        return pltpu.make_async_remote_copy(
            src_ref=mine, dst_ref=gathered.at[me],
            send_sem=fit_send.at[partner], recv_sem=fit_recv.at[me],
            device_id={"ccd": partner}, device_id_type=MESH,
        )

    @pl.loop(1, n)
    def _(i):
        share(i).start()

    @pl.loop(1, n)
    def _(i):
        share(i).wait_send()
        source = lax.rem(me + n - i, n)
        pltpu.make_async_remote_copy(
            src_ref=mine, dst_ref=gathered.at[source],
            send_sem=fit_send.at[source], recv_sem=fit_recv.at[source],
            device_id={"ccd": source}, device_id_type=MESH,
        ).wait_recv()

    system = lax.fori_loop(
        0, n, lambda j, total: total + gathered[j], jnp.zeros((32, BC), jnp.float32)
    )
    diagonal = (row_id == lane_id) & (row_id < KB)
    trace = jnp.sum(jnp.where(diagonal, system, 0.0), keepdims=True)
    ridge = 0.001 * trace / KB + 1.0
    system = system + jnp.where(diagonal, jnp.broadcast_to(ridge, (32, BC)), 0.0)
    for k in range(KB):
        pivot = system[k : k + 1, :] / system[k : k + 1, k : k + 1]
        system = jnp.where(row_id == k, pivot, system - system[:, k : k + 1] * pivot)
    for i in range(KB):
        weights[i] = jnp.broadcast_to(system[i : i + 1, KB : KB + 1], (8, BC))

    @pl.loop(0, groups)
    def _(g):
        start = pl.multiple_of(g * 8, 8)
        for lb in range(lanes):
            model = None
            for r in range(KSIDE):
                for q in range(KSIDE):
                    term = weights[r * KSIDE + q] * basis[q, lb, pl.ds(start + r, 8), :]
                    model = term if model is None else model + term
            out_ref[pl.ds(start, 8), lb * BC : (lb + 1) * BC] = (
                s_ref[lb, pl.ds(start, 8), :] - model
            )


def body(exposures, lanczos_shift, lanczos_frac, margin_patch, margin_slot):
    rows, columns = exposures.shape[1], exposures.shape[2]
    lanes, bands = columns // BC, rows // BR
    n = lax.axis_size("ccd")
    me = lax.axis_index("ccd")
    cap = max(2, 2 * NB // n)
    vmem = pl.BlockSpec(memory_space=pltpu.VMEM)
    smem = pl.BlockSpec(memory_space=pltpu.SMEM)
    f32 = jnp.float32

    steps = jnp.arange(LOW, HIGH + 1).astype(f32)
    offset = steps - lanczos_shift[:, 0, :, None].astype(f32) - lanczos_frac[:, 0, :, None]
    taps = jnp.where(
        jnp.abs(offset) < 3.0, jnp.sinc(offset) * jnp.sinc(offset / 3.0), jnp.zeros_like(offset)
    )

    targets = margin_patch[:, :, 0]
    ids = jnp.arange(NB)
    same = targets[:, :, None] == targets[:, None, :]
    order = jnp.sum(same & (ids[None, :] < ids[:, None])[None], axis=2)
    my_targets = lax.dynamic_slice_in_dim(targets, me, 1, 0)[0]
    my_order = lax.dynamic_slice_in_dim(order, me, 1, 0)[0]
    lane_major = (ids % lanes) * bands + ids // lanes
    key = my_targets * cap + my_order
    index = jnp.sum(
        jnp.where(key[None, :] == jnp.arange(n * cap)[:, None], lane_major[None, :], 0), axis=1
    ).astype(jnp.int32)
    arrives = (targets == me)[:, None, :] & (order[:, None, :] == jnp.arange(cap)[None, :, None])
    spots = (margin_slot % lanes) * bands + margin_slot // lanes
    place = (
        NB + jnp.sum(jnp.where(arrives, spots[:, None, :] - NB, 0), axis=2)
    ).reshape(n * cap).astype(jnp.int32)

    got = pl.pallas_call(
        functools.partial(exchange_kernel, n, cap),
        out_shape=jax.ShapeDtypeStruct((2, n, cap, BR, BC), f32),
        in_specs=[smem, smem, vmem],
        out_specs=vmem,
        scratch_shapes=[
            pltpu.VMEM((lanes, rows + 16, BC), f32),
            pltpu.VMEM((2, NB, BR, BC), f32),
            pltpu.VMEM((2, n, cap, BR, BC), f32),
            pltpu.SemaphoreType.DMA((2, n)),
            pltpu.SemaphoreType.DMA((2, n)),
            pltpu.SemaphoreType.DMA((2,)),
        ],
        compiler_params=pltpu.CompilerParams(
            collective_id=0, has_side_effects=True, vmem_limit_bytes=VMEM_LIMIT
        ),
        name="warp_exchange",
    )(taps, index, exposures)

    pile = jax.ShapeDtypeStruct((NB + 1, BR, BC), f32)
    template, science = pl.pallas_call(
        functools.partial(coadd_kernel, n * cap),
        out_shape=(pile, pile),
        in_specs=[smem, vmem],
        out_specs=(vmem, vmem),
        compiler_params=pltpu.CompilerParams(vmem_limit_bytes=VMEM_LIMIT),
        name="coadd",
    )(place, got.reshape(2, n * cap, BR, BC))
    template = template[:NB].reshape(lanes, rows, BC)
    science = science[:NB].reshape(lanes, rows, BC)

    return pl.pallas_call(
        functools.partial(fit_kernel, n),
        out_shape=jax.ShapeDtypeStruct((rows, columns), f32),
        in_specs=[vmem, vmem],
        out_specs=vmem,
        scratch_shapes=[
            pltpu.VMEM((lanes, 8, BC), f32),
            pltpu.VMEM((lanes, 8, BC), f32),
            pltpu.VMEM((KSIDE, lanes, rows + 16, BC), f32),
            pltpu.VMEM((KB + 1, 32, BC), f32),
            pltpu.VMEM((32, BC), f32),
            pltpu.VMEM((n, 32, BC), f32),
            pltpu.VMEM((KB, 8, BC), f32),
            pltpu.SemaphoreType.DMA((2,)),
            pltpu.SemaphoreType.DMA((2,)),
            pltpu.SemaphoreType.DMA((n,)),
            pltpu.SemaphoreType.DMA((n,)),
        ],
        compiler_params=pltpu.CompilerParams(
            collective_id=1, has_side_effects=True, vmem_limit_bytes=VMEM_LIMIT
        ),
        name="fit_subtract",
    )(template, science)


def solution(mesh):
    placed = (
        P(None, ("field", "ccd"), None),
        P(None, ("field", "ccd"), None),
        P(None, ("field", "ccd"), None),
        P("field", None, None),
        P("field", None),
    )
    return jax.shard_map(
        body, mesh=mesh, in_specs=placed, out_specs=P(("field", "ccd"), None), check_vma=False
    )
```

```python
import functools

import jax
import jax.numpy as jnp
from jax import lax
from jax.experimental import pallas as pl
from jax.experimental.pallas import tpu as pltpu
from jax.sharding import PartitionSpec as P

BR = 32
BC = 128
KSIDE = 5
KB = 25
NB = 32
REACH = KSIDE // 2
LOW, HIGH = -4, 5
TAPS = HIGH - LOW + 1
MESH = pl.DeviceIdType.MESH
VMEM_LIMIT = 56 * 1024 * 1024


def greet_all(n, me):
    barrier = pltpu.get_barrier_semaphore()

    @pl.loop(1, n)
    def _(i):
        pl.semaphore_signal(
            barrier, inc=1, device_id={"ccd": lax.rem(me + i, n)}, device_id_type=MESH
        )

    return barrier


def sinc(x):
    scaled = jnp.pi * jnp.where(x == 0.0, 1.0, x)
    return jnp.where(x == 0.0, 1.0, jnp.sin(scaled) / scaled)


def share_part(n, me, part, mine, gathered, send_sem, recv_sem):
    mine[...] = part
    gathered[me] = part

    def share(i):
        partner = lax.rem(me + i, n)
        return pltpu.make_async_remote_copy(
            src_ref=mine, dst_ref=gathered.at[me],
            send_sem=send_sem.at[partner], recv_sem=recv_sem.at[me],
            device_id={"ccd": partner}, device_id_type=MESH,
        )

    @pl.loop(1, n)
    def _(i):
        share(i).start()

    @pl.loop(1, n)
    def _(i):
        share(i).wait_send()
        source = lax.rem(me + n - i, n)
        pltpu.make_async_remote_copy(
            src_ref=mine, dst_ref=gathered.at[source],
            send_sem=send_sem.at[source], recv_sem=recv_sem.at[source],
            device_id={"ccd": source}, device_id_type=MESH,
        ).wait_recv()

    return lax.fori_loop(
        0, n, lambda j, total: total + gathered[j], jnp.zeros((32, BC), jnp.float32)
    )


def whole_kernel(n, cap, shift_ref, frac_ref, index_ref, prev_ref, chain_ref, last_ref, any_ref,
                 raw_ref, out_ref, taps, rows_pad, warped, send, got, run, t_img, s_img, top, low,
                 basis, entries, products, mine, gathered, weights, send_sem, recv_sem, own_sem,
                 halo_send, halo_recv, fit_send, fit_recv):
    me = lax.axis_index("ccd")
    barrier = greet_all(n, me)
    rows, columns = raw_ref.shape[1:]
    lanes, bands, groups = columns // BC, rows // BR, rows // 8
    width = columns + BC
    right, left = lax.rem(me + 1, n), lax.rem(me + n - 1, n)
    rows_pad[:, 0:8, :] = jnp.zeros((lanes, 8, BC), jnp.float32)
    rows_pad[:, rows + 8 : rows + 16, :] = jnp.zeros((lanes, 8, BC), jnp.float32)
    entries[...] = jnp.zeros_like(entries)
    products[...] = jnp.zeros_like(products)

    steps = lax.broadcasted_iota(jnp.int32, (8, BC), 1) + LOW
    for v in range(2):
        for axis in range(2):
            offset = (steps - shift_ref[v, 0, axis]).astype(jnp.float32) - frac_ref[v, 0, axis]
            taper = jnp.where(jnp.abs(offset) < 3.0, sinc(offset) * sinc(offset / 3.0), 0.0)
            for k in range(TAPS):
                taps[v, axis, k] = jnp.broadcast_to(taper[:, k : k + 1], (8, BC))

    def copy_to(v, i):
        partner = lax.rem(me + i, n)
        return pltpu.make_async_remote_copy(
            src_ref=send.at[v, partner], dst_ref=got.at[v, me],
            send_sem=send_sem.at[v, partner], recv_sem=recv_sem.at[v, me],
            device_id={"ccd": partner}, device_id_type=MESH,
        )

    def own_copy(v):
        return pltpu.make_async_copy(send.at[v, me], got.at[v, me], own_sem.at[v])

    def shifted(pieces, low_step, high_step):
        line = jnp.concatenate(pieces + [jnp.zeros((8, BC), jnp.float32)], axis=1)
        for k in range(low_step, high_step + 1):
            yield k - low_step, line if k == 0 else pltpu.roll(line, (-k) % width, 1)

    for v in range(2):

        @pl.loop(0, groups)
        def _(c):
            start = pl.multiple_of(c * 8, 8)
            totals = [None] * lanes
            for k, line in shifted([raw_ref[v, pl.ds(start, 8), :]], LOW, HIGH):
                tap = taps[v, 1, k]
                for lb in range(lanes):
                    term = tap * line[:, lb * BC : (lb + 1) * BC]
                    totals[lb] = term if k == 0 else totals[lb] + term
            for lb in range(lanes):
                rows_pad[lb, pl.ds(start + 8, 8), :] = totals[lb]

        @pl.loop(0, lanes)
        def _(lb):
            for rb in range(bands):
                totals = [None] * (BR // 8)
                for k in range(TAPS):
                    tap = taps[v, 0, k]
                    for i in range(BR // 8):
                        first = 8 + rb * BR + i * 8 + k + LOW
                        term = tap * rows_pad[lb, first : first + 8, :]
                        totals[i] = term if k == 0 else totals[i] + term
                for i in range(BR // 8):
                    warped[v, lb * bands + rb, i * 8 : (i + 1) * 8, :] = totals[i]

        @pl.loop(0, n)
        def _(p):
            for z in range(cap):
                send[v, p, z] = warped[v, index_ref[p * cap + z]]

        if v == 0:
            pl.semaphore_wait(barrier, n - 1)

        @pl.loop(1, n)
        def _(i):
            if v == 1:
                copy_to(0, i).wait_send()
            copy_to(v, i).start()

        own_copy(v).start()

    def receive(v, image):
        own_copy(v).wait()

        @pl.loop(1, n)
        def _(i):
            if v == 1:
                copy_to(v, i).wait_send()
            source = lax.rem(me + n - i, n)
            pltpu.make_async_remote_copy(
                src_ref=send.at[v, source], dst_ref=got.at[v, source],
                send_sem=send_sem.at[v, source], recv_sem=recv_sem.at[v, source],
                device_id={"ccd": source}, device_id_type=MESH,
            ).wait_recv()

        run[0] = got[v, 0, 0]
        for z in range(1, cap):
            run[z] = got[v, 0, z] + chain_ref[z] * run[prev_ref[z]]

        @pl.loop(1, n)
        def _(f):
            for z in range(cap):
                t = f * cap + z
                run[t] = got[v, f, z] + chain_ref[t] * run[prev_ref[t]]

        @pl.loop(0, lanes)
        def _(lb):
            for rb in range(bands):
                e = lb * bands + rb
                image[lb, rb * BR : (rb + 1) * BR, :] = any_ref[e] * run[last_ref[e]]

    run[...] = jnp.zeros_like(run)
    receive(0, t_img)

    down = pltpu.make_async_remote_copy(
        src_ref=t_img.at[:, pl.ds(rows - 8, 8), :], dst_ref=top,
        send_sem=halo_send.at[0], recv_sem=halo_recv.at[0],
        device_id={"ccd": right}, device_id_type=MESH,
    )
    up = pltpu.make_async_remote_copy(
        src_ref=t_img.at[:, pl.ds(0, 8), :], dst_ref=low,
        send_sem=halo_send.at[1], recv_sem=halo_recv.at[1],
        device_id={"ccd": left}, device_id_type=MESH,
    )
    down.start()
    up.start()

    @pl.loop(0, groups)
    def _(g):
        start = pl.multiple_of(g * 8, 8)
        pieces = [t_img[lb, pl.ds(start, 8), :] for lb in range(lanes)]
        for q, line in shifted(pieces, -REACH, REACH):
            for lb in range(lanes):
                basis[q, lb, pl.ds(start + REACH, 8), :] = line[:, lb * BC : (lb + 1) * BC]

    down.wait()
    up.wait()
    has_top = (me > 0).astype(jnp.float32)
    has_low = (me < n - 1).astype(jnp.float32)
    for q, line in shifted([top[lb] * has_top for lb in range(lanes)], -REACH, REACH):
        for lb in range(lanes):
            basis[q, lb, 0:REACH, :] = line[8 - REACH : 8, lb * BC : (lb + 1) * BC]
    first = rows + REACH
    for q, line in shifted([low[lb] * has_low for lb in range(lanes)], -REACH, REACH):
        for lb in range(lanes):
            basis[q, lb, first : first + REACH, :] = line[0:REACH, lb * BC : (lb + 1) * BC]
            basis[q, lb, first + REACH : rows + 16, :] = jnp.zeros(
                (16 - 2 * REACH, BC), jnp.float32
            )

    sub = lax.broadcasted_iota(jnp.int32, (8, BC), 0)
    nothing = (jnp.zeros((8, BC), jnp.float32),) * KSIDE

    for dr in range(KSIDE):

        @pl.loop(0, KSIDE)
        def _(qq):
            def add(start, sums):
                sums = list(sums)
                for lb in range(lanes):
                    other = basis[qq, lb, pl.ds(start + dr, 8), :]
                    for q in range(KSIDE):
                        sums[q] = sums[q] + basis[q, lb, pl.ds(start, 8), :] * other
                return tuple(sums)

            head = add(0, nothing)
            core = lax.fori_loop(
                1, groups, lambda g, sums: add(pl.multiple_of(g * 8, 8), sums), nothing
            )
            tail = add(rows, nothing)
            for r in range(KSIDE - dr):
                for q in range(KSIDE):
                    window = (
                        core[q]
                        + jnp.where(sub >= r, head[q], 0.0)
                        + jnp.where(sub < r, tail[q], 0.0)
                    )
                    line = jnp.sum(window, 0, keepdims=True)
                    here = (r + dr) * KSIDE + qq
                    entries[here, r * KSIDE + q : r * KSIDE + q + 1, :] = line
                    if dr > 0:
                        entries[r * KSIDE + q, pl.ds(here, 1), :] = line

    row_id = lax.broadcasted_iota(jnp.int32, (32, BC), 0)
    lane_id = lax.broadcasted_iota(jnp.int32, (32, BC), 1)
    part = jnp.zeros((32, BC), jnp.float32)
    for j in range(KB):
        part = jnp.where(lane_id == j, jnp.sum(entries[j], 1, keepdims=True), part)
    gram = share_part(n, me, part, mine.at[0], gathered.at[0], fit_send.at[0], fit_recv.at[0])
    diagonal = (row_id == lane_id) & (row_id < KB)
    trace = jnp.sum(jnp.where(diagonal, gram, 0.0), keepdims=True)
    ridge = 0.001 * trace / KB + 1.0
    gram = gram + jnp.where(diagonal, jnp.broadcast_to(ridge, (32, BC)), 0.0)
    half = BC // 2
    system = gram + jnp.where((row_id + half == lane_id) & (row_id < KB), 1.0, 0.0)
    for k in range(KB):
        pivot = system[k : k + 1, :] / system[k : k + 1, k : k + 1]
        system = jnp.where(row_id == k, pivot, system - system[:, k : k + 1] * pivot)
    inverse = jnp.where(lane_id < KB, pltpu.roll(system, half, 1), 0.0)

    receive(1, s_img)

    for r in range(KSIDE):

        def add(g, sums):
            start = pl.multiple_of(g * 8, 8)
            sums = list(sums)
            for lb in range(lanes):
                target = s_img[lb, pl.ds(start, 8), :]
                for q in range(KSIDE):
                    sums[q] = sums[q] + basis[q, lb, pl.ds(start + r, 8), :] * target
            return tuple(sums)

        sums = lax.fori_loop(0, groups, add, nothing)
        for q in range(KSIDE):
            i = r * KSIDE + q
            products[i : i + 1, :] = jnp.sum(sums[q], 0, keepdims=True)

    summed = share_part(
        n, me, products[...], mine.at[1], gathered.at[1], fit_send.at[1], fit_recv.at[1]
    )
    rhs = jnp.sum(summed, 1, keepdims=True)
    solved = jnp.sum(inverse * rhs, 0, keepdims=True)
    residual = rhs - jnp.sum(gram * solved, 1, keepdims=True)
    solved = solved + jnp.sum(inverse * residual, 0, keepdims=True)
    for i in range(KB):
        weights[i] = jnp.broadcast_to(solved[:, i : i + 1], (8, BC))

    @pl.loop(0, groups)
    def _(g):
        start = pl.multiple_of(g * 8, 8)
        models = [None] * lanes
        for r in range(KSIDE):
            for q in range(KSIDE):
                weight = weights[r * KSIDE + q]
                for lb in range(lanes):
                    term = weight * basis[q, lb, pl.ds(start + r, 8), :]
                    models[lb] = term if models[lb] is None else models[lb] + term
        for lb in range(lanes):
            out_ref[pl.ds(start, 8), lb * BC : (lb + 1) * BC] = (
                s_img[lb, pl.ds(start, 8), :] - models[lb]
            )


def body(exposures, lanczos_shift, lanczos_frac, margin_patch, margin_slot):
    rows, columns = exposures.shape[1], exposures.shape[2]
    lanes, bands = columns // BC, rows // BR
    n = lax.axis_size("ccd")
    me = lax.axis_index("ccd")
    cap = max(2, 2 * NB // n)
    vmem = pl.BlockSpec(memory_space=pltpu.VMEM)
    smem = pl.BlockSpec(memory_space=pltpu.SMEM)
    f32 = jnp.float32

    targets = margin_patch[:, :, 0]
    ids = jnp.arange(NB)
    same = targets[:, :, None] == targets[:, None, :]
    order = jnp.sum(same & (ids[None, :] < ids[:, None])[None], axis=2)
    my_targets = lax.dynamic_slice_in_dim(targets, me, 1, 0)[0]
    my_order = lax.dynamic_slice_in_dim(order, me, 1, 0)[0]
    lane_major = (ids % lanes) * bands + ids // lanes
    key = my_targets * cap + my_order
    index = jnp.sum(
        jnp.where(key[None, :] == jnp.arange(n * cap)[:, None], lane_major[None, :], 0), axis=1
    ).astype(jnp.int32)
    arrives = (targets == me)[:, None, :] & (order[:, None, :] == jnp.arange(cap)[None, :, None])
    spots = (margin_slot % lanes) * bands + margin_slot // lanes
    count = n * cap
    spot = NB + jnp.sum(jnp.where(arrives, spots[:, None, :] - NB, 0), axis=2).reshape(count)
    turns = jnp.arange(count)
    matches = (spot[None, :] == spot[:, None]) & (spot[:, None] < NB)
    prev = jnp.max(
        jnp.where(matches & (turns[None, :] < turns[:, None]), turns[None, :], -1), axis=1
    ).astype(jnp.int32)
    last = jnp.max(
        jnp.where(spot[None, :] == ids[:, None], turns[None, :], -1), axis=1
    ).astype(jnp.int32)
    chain, filled = (prev >= 0).astype(f32), (last >= 0).astype(f32)
    prev, last = jnp.maximum(prev, 0), jnp.maximum(last, 0)

    return pl.pallas_call(
        functools.partial(whole_kernel, n, cap),
        out_shape=jax.ShapeDtypeStruct((rows, columns), f32),
        in_specs=[smem] * 7 + [vmem],
        out_specs=vmem,
        scratch_shapes=[
            pltpu.VMEM((2, 2, TAPS, 8, BC), f32),
            pltpu.VMEM((lanes, rows + 16, BC), f32),
            pltpu.VMEM((2, NB, BR, BC), f32),
            pltpu.VMEM((2, n, cap, BR, BC), f32),
            pltpu.VMEM((2, n, cap, BR, BC), f32),
            pltpu.VMEM((count, BR, BC), f32),
            pltpu.VMEM((lanes, rows, BC), f32),
            pltpu.VMEM((lanes, rows, BC), f32),
            pltpu.VMEM((lanes, 8, BC), f32),
            pltpu.VMEM((lanes, 8, BC), f32),
            pltpu.VMEM((KSIDE, lanes, rows + 16, BC), f32),
            pltpu.VMEM((KB, 32, BC), f32),
            pltpu.VMEM((32, BC), f32),
            pltpu.VMEM((2, 32, BC), f32),
            pltpu.VMEM((2, n, 32, BC), f32),
            pltpu.VMEM((KB, 8, BC), f32),
            pltpu.SemaphoreType.DMA((2, n)),
            pltpu.SemaphoreType.DMA((2, n)),
            pltpu.SemaphoreType.DMA((2,)),
            pltpu.SemaphoreType.DMA((2,)),
            pltpu.SemaphoreType.DMA((2,)),
            pltpu.SemaphoreType.DMA((2, n)),
            pltpu.SemaphoreType.DMA((2, n)),
        ],
        compiler_params=pltpu.CompilerParams(
            collective_id=0, has_side_effects=True, vmem_limit_bytes=VMEM_LIMIT
        ),
        name="difference",
    )(lanczos_shift, lanczos_frac, index, prev, chain, last, filled, exposures)


def solution(mesh):
    placed = (
        P(None, ("field", "ccd"), None),
        P(None, ("field", "ccd"), None),
        P(None, ("field", "ccd"), None),
        P("field", None, None),
        P("field", None),
    )
    return jax.shard_map(
        body, mesh=mesh, in_specs=placed, out_specs=P(("field", "ccd"), None), check_vma=False
    )
```
